32 devices in a mesh: groups: 2 (over y), leaf: 4 (over x, core), vec: 4 (over z).
Axes of the slice: x: 2, y: 2, z: 4, core: 2. Of those that a mesh axis runs over, the one named last changes fastest.
Arguments:
- vectors: float32 [16, 65536], P('vec', ('groups', 'leaf')), parts along dimension 1, may hold values from -6 to 6
- coords: float32 [3, 65536], P(None, ('groups', 'leaf')), parts along dimension 1, may hold values from -1 to 1
- weights: float32 [65536], P(('groups', 'leaf')), parts along dimension 0, may hold values from 0.05 to 0.5
- basis: float32 [512, 64, 128], P(('groups', 'leaf')), parts along dimension 0, may hold values from -0.5 to 0.5
- transfer: float32 [8, 64, 64], replicated, may hold values from -0.25 to 0.25
- coupling: float32 [316, 64, 64], replicated, may hold values from -0.0625 to 0.0625
- far_leaf: int32 [512, 316], P(('groups', 'leaf')), parts along dimension 0, may hold values from -1 to 255, as said below
- far_parent: int32 [64, 316], P(('groups', 'leaf')), parts along dimension 0, may hold values from -1 to 31, as said below
- near_leaf: int32 [512, 27], P(('groups', 'leaf')), parts along dimension 0, may hold values from -1 to 255, as said below
Outputs:
- product: float32 [16, 65536], P('vec', ('groups', 'leaf')), parts along dimension 1
The draws below stay inside these ranges and needn't reach their ends.
There are 2 independent parts, one for each index of `groups`. The reference program is written for one: setup_inputs(seed, part) draws one part's arguments, and reference() takes and returns one part's arrays. A program takes and returns all parts, laid end to end along the dimension named above; an argument that names none is the same for every part. Nothing has to cross between parts.
Inputs may be any that keep to these rules, and one draw needn't show every extreme that they name: `far_leaf`: -1 marks an empty slot; a live entry names a leaf among the 64 leaves of the same block of 64 leaves as l or of the block just before or after it. `near_leaf`: -1 marks an empty slot; a live entry names a leaf among the 64 leaves of the same block of 64 leaves as l or of the block just before or after it. `far_parent`: -1 marks an empty slot; a live entry names a parent of the same block of 8 parents as q or of the block just before or after it.
All inputs are finite; a program needn't handle non-finite values.
Results may differ from the reference program's by a relative error of at most 0.0003.
Values sent between devices are 32-bit elements; how exact they have to be, the bound alone decides.
A program may use at most 64 MiB of HBM per device.

```python
import math
import jax
import jax.numpy as jnp
from jax import lax

NV = 16
LEAF = 128
R = 64
NOFF = 316
KN = 27
LD = 64
NL = 256
NPAR = 32
NP = 32768


def window_partners(key, count, slots, block, live_tenths):
    leaf_ids = jnp.arange(count, dtype=jnp.int32)[:, None]
    owner = leaf_ids // block
    blocks = count // block
    lower = jnp.maximum(owner - 1, 0) * block
    upper = jnp.minimum(owner + 2, blocks) * block
    key_pick, key_live = jax.random.split(key)
    raw = jax.random.randint(key_pick, (count, slots), 0, 1 << 20)
    partner = lower + raw % (upper - lower)
    live = jax.random.randint(key_live, (count, slots), 0, 10) < live_tenths
    partner = jnp.where(live, partner, -1).astype(jnp.int32)
    partner = partner.at[count - 2, 0].set(count - 1)
    partner = partner.at[0, 1].set(-1)
    return partner


def draw_far_leaf(key, part):
    key = jax.random.fold_in(key, 11)
    return window_partners(key, NL, NOFF, LD, 6)


def draw_near_leaf(key, part):
    key = jax.random.fold_in(key, 12)
    return window_partners(key, NL, KN, LD, 8)


def draw_far_parent(key, part):
    key = jax.random.fold_in(key, 13)
    return window_partners(key, NPAR, NOFF, LD // 8, 6)


def steps_of(own_key, extent, cuts, smallest, top_value):
    gain = 1.0
    for axis_at, parts in cuts:
        draws = jax.random.uniform(jax.random.fold_in(jax.random.fold_in(own_key, 6), axis_at), (parts,), jnp.float32, smallest / len(cuts), top_value / len(cuts))
        gain = gain * jnp.repeat(jnp.exp(draws), extent[axis_at] // parts).reshape((-1,) + (1,) * (len(extent) - 1 - axis_at))
    return gain


def noise(rng, shape, scale, most, pieces=(), kind=jnp.bfloat16):
    array = scale * jax.random.normal(rng, shape, jnp.float32)
    if pieces:
        array = array * steps_of(rng, shape, pieces, -0.22, 0.18)
    return jnp.clip(array, -most, most).astype(kind)


def setup_inputs(seed: int = 0, part: int = 0) -> dict:
    keys = jax.random.split(jax.random.key(seed), 10)
    own_keys = jax.random.split(jax.random.fold_in(keys[9], part), 10)
    vectors = noise(own_keys[0], (NV, NP), 1.0, 6.0, ((0, 4), (1, 4)), jnp.float32)
    coords = jnp.clip(jax.random.uniform(own_keys[1], (3, NP), jnp.float32, -1.0, 1.0) * steps_of(own_keys[1], (3, NP), ((1, 4),), -0.4, 0.0), -1.0, 1.0)
    weights = jnp.clip(jnp.exp(math.log(0.5) - 2.3025851 * jax.random.uniform(own_keys[2], (NP,), jnp.float32) ** steps_of(own_keys[2], (NP,), ((0, 4),), -0.2, 0.2)), 0.05, 0.5)
    basis = noise(own_keys[3], (NL, R, LEAF), LEAF ** -0.5, 0.5, ((0, 4),), jnp.float32)
    transfer = noise(keys[4], (8, R, R), (8 * R) ** -0.5, 0.25, (), jnp.float32)
    coupling = noise(keys[5], (NOFF, R, R), (R * NOFF // 2) ** -0.5, 0.0625, (), jnp.float32)
    far_leaf = draw_far_leaf(jax.random.fold_in(jax.random.fold_in(keys[9], part), 71), part)
    far_parent = draw_far_parent(jax.random.fold_in(jax.random.fold_in(keys[9], part), 71), part)
    near_leaf = draw_near_leaf(jax.random.fold_in(jax.random.fold_in(keys[9], part), 71), part)
    return dict(vectors=vectors, coords=coords, weights=weights, basis=basis, transfer=transfer, coupling=coupling, far_leaf=far_leaf, far_parent=far_parent, near_leaf=near_leaf)


HI = lax.Precision.HIGHEST
SOFT_SQ = 0.0001

def couple(source, lists, coupling):
    count = lists.shape[0]
    blk = math.gcd(count, 8)

    def one(part_lists):
        mask = (part_lists >= 0).astype(coupling.dtype)
        picked = source[jnp.maximum(part_lists, 0)] * mask[:, :, None, None]
        return jnp.einsum('ors,novs->nvr', coupling, picked, precision=HI)
    result = lax.map(one, lists.reshape(count // blk, blk, lists.shape[1]))
    return result.reshape(count, source.shape[1], source.shape[2])

def near_field(target_co, source_co, source_wx, lists):
    count = lists.shape[0]
    width = target_co.shape[2]
    nvec = source_wx.shape[0]
    blk = math.gcd(count, 8)

    def one(args):
        tco, part_lists = args
        mask = (part_lists >= 0).astype(source_co.dtype)
        safe = jnp.maximum(part_lists, 0)
        sco = source_co[:, safe]
        swx = source_wx[:, safe]
        diff = tco[:, :, None, :, None] - sco[:, :, :, None, :]
        dist_sq = lax.optimization_barrier(jnp.sum(diff * diff, axis=0))
        kernel = mask[:, :, None, None] / (4.0 * jnp.pi * jnp.sqrt(dist_sq + SOFT_SQ))
        return jnp.einsum('bkpq,vbkq->vbp', kernel, swx, precision=HI)
    blocks_co = target_co.reshape(3, count // blk, blk, width).transpose(1, 0, 2, 3)
    blocks_lists = lists.reshape(count // blk, blk, lists.shape[1])
    result = lax.map(one, (blocks_co, blocks_lists))
    return result.transpose(1, 0, 2, 3).reshape(nvec, count, width)

def reference(vectors, coords, weights, basis, transfer, coupling, far_leaf, far_parent, near_leaf):
    nvec = vectors.shape[0]
    leaf_x = vectors.reshape(nvec, NL, LEAF)
    coeff = jnp.einsum('lrp,vlp->lvr', basis, leaf_x, precision=HI)
    parent = jnp.einsum('jrs,qjvs->qvr', transfer, coeff.reshape(NPAR, 8, nvec, R), precision=HI)
    far_par = 0.5 * couple(parent, far_parent, coupling)
    down = jnp.einsum('jsr,qvs->qjvr', transfer, far_par, precision=HI).reshape(NL, nvec, R)
    local = couple(coeff, far_leaf, coupling) + down
    far_out = jnp.einsum('lrp,lvr->vlp', basis, local, precision=HI)
    weighted = (vectors * weights[None, :]).reshape(nvec, NL, LEAF)
    leaf_co = coords.reshape(3, NL, LEAF)
    near_out = near_field(leaf_co, leaf_co, weighted, near_leaf)
    return (far_out + near_out).reshape(nvec, NP)
```

```python
import functools
import math

import jax
import jax.numpy as jnp
from jax import lax
from jax.experimental import pallas as pl
from jax.experimental.pallas import tpu as pltpu
from jax.sharding import PartitionSpec as P

SOFT_SQ = 0.0001
F32 = jnp.float32
BF16 = jnp.bfloat16
VMEM_BYTES = 48 * 1024 * 1024
NT = (((1,), (1,)), ((), ()))
NN = (((1,), (0,)), ((), ()))


def split(x):
    hi = x.astype(BF16)
    lo = (x - hi.astype(F32)).astype(BF16)
    return hi, lo


def dot(a, b, dims):
    return lax.dot_general(a, b, dims, preferred_element_type=F32)


def dot3(a, b, dims):
    ahi, alo = split(a)
    bhi, blo = split(b)
    return dot(ahi, bhi, dims) + dot(ahi, blo, dims) + dot(alo, bhi, dims)


def twice_diag(c):
    z = jnp.zeros_like(c)
    return jnp.concatenate(
        [jnp.concatenate([c, z], axis=1), jnp.concatenate([z, c], axis=1)], axis=0
    )


def up_kernel(x_ref, basis_ref, out_ref):
    nleaf, nvec, _ = x_ref.shape
    rank = basis_ref.shape[1]

    def step(leaf, carry):
        x = x_ref[leaf]
        xhi = x.astype(BF16).astype(F32)
        lhs = jnp.concatenate([xhi, x - xhi], axis=0).astype(BF16)
        bhi, blo = split(basis_ref[leaf])
        r = dot(lhs, jnp.concatenate([bhi, blo], axis=0), NT)
        out_ref[leaf] = r[:nvec, :rank] + r[nvec:, :rank] + r[:nvec, rank:]
        return carry

    lax.fori_loop(0, nleaf, step, 0, unroll=8)


def far_kernel(
    left_ref, mid_ref, right_ref, transfer_ref, coupling_ref, idx_ref, basis_ref,
    out_ref, all_ref, src_ref, loc_ref,
):
    nleaf, cols = mid_ref.shape
    nvec = out_ref.shape[0]
    rank = basis_ref.shape[1]
    npair = cols // 128
    nsrc = 3 * nleaf
    npar = nleaf // 8
    rows = idx_ref.shape[1]
    per = idx_ref.shape[2]
    depth = src_ref.shape[0]

    for p in range(npair):
        at = slice(p * 128, (p + 1) * 128)
        all_ref[p, :nleaf] = left_ref[:, at]
        all_ref[p, nleaf : 2 * nleaf] = mid_ref[:, at]
        all_ref[p, 2 * nleaf : nsrc] = right_ref[:, at]
        all_ref[p, nsrc:depth] = jnp.zeros((depth - nsrc, 128), F32)
    par = [jnp.zeros((3 * npar, 128), F32) for _ in range(npair)]
    for j in range(8):
        w = twice_diag(transfer_ref[j])
        for p in range(npair):
            c = all_ref[p, pl.ds(j, 3 * npar, stride=8), :]
            par[p] = par[p] + dot3(c, w, NT)
    for p in range(npair):
        all_ref[p, nsrc : nsrc + 3 * npar] = par[p]
        hi, lo = split(all_ref[p])
        src_ref[:, p * 128 : (p + 1) * 128] = hi
        src_ref[:, cols + p * 128 : cols + (p + 1) * 128] = lo

    lane = lax.broadcasted_iota(jnp.int32, (rows, depth), 1)

    def couple(i, acc):
        acc_a, acc_b = acc
        idx = idx_ref[i]
        hot = [
            jnp.where(idx[:, j : j + 1] == lane, 1.0, 0.0).astype(BF16) for j in range(per)
        ]
        got = dot(jnp.concatenate(hot, axis=0), src_ref[...], NN).astype(BF16)
        for h in range(per // 2):
            whi, wlo = [], []
            for j in (2 * h, 2 * h + 1):
                c = coupling_ref[i * per + j]
                chi, clo = split(twice_diag(c))
                whi.append(chi)
                wlo.append(clo)
            whi = jnp.concatenate(whi, axis=1)
            wlo = jnp.concatenate(wlo, axis=1)
            w = jnp.concatenate([whi, wlo], axis=0)

            def take(start):
                return jnp.concatenate(
                    [
                        jnp.concatenate(
                            [
                                got[j * rows : (j + 1) * rows, start + p * 128 : start + (p + 1) * 128]
                                for j in (2 * h, 2 * h + 1)
                            ],
                            axis=1,
                        )
                        for p in range(npair)
                    ],
                    axis=0,
                )

            acc_a = acc_a + dot(take(0), w, NT)
            acc_b = acc_b + dot(take(cols), whi, NT)
        return acc_a, acc_b

    acc_a, acc_b = lax.fori_loop(
        0,
        idx_ref.shape[0],
        couple,
        (jnp.zeros((npair * rows, 256), F32), jnp.zeros((npair * rows, 128), F32)),
    )
    total = acc_a[:, :128] + acc_a[:, 128:] + acc_b
    for p in range(npair):
        loc_ref[p] = total[p * rows : p * rows + nleaf]
    for j in range(8):
        w = twice_diag(transfer_ref[j])
        for p in range(npair):
            far = 0.5 * total[p * rows + nleaf : p * rows + nleaf + npar]
            at = (p, pl.ds(j, npar, stride=8), slice(None))
            loc_ref[at] = loc_ref[at] + dot3(far, w, NN)

    low = lax.broadcasted_iota(jnp.int32, (1, 128), 1) < rank

    def leaf_out(leaf, carry):
        parts = []
        for p in range(npair):
            piece = loc_ref[p, pl.ds(leaf, 1), :]
            parts.append(jnp.where(low, piece, 0.0))
            parts.append(jnp.where(low, 0.0, piece))
        lhs = jnp.concatenate(parts, axis=0)
        lhi = lhs.astype(BF16).astype(F32)
        lhs = jnp.concatenate([lhi, lhs - lhi], axis=0).astype(BF16)
        bhi, blo = split(basis_ref[leaf])
        b = jnp.concatenate([bhi, blo], axis=1)
        r = dot(lhs, jnp.concatenate([b, b], axis=0), NN)
        out_ref[:, pl.ds(pl.multiple_of(leaf * 128, 128), 128)] = (
            r[:nvec, :128] + r[nvec:, :128] + r[:nvec, 128:]
        )
        return carry

    lax.fori_loop(0, nleaf, leaf_out, 0, unroll=8)


def near_kernel(
    list_ref, co_l, co_m, co_r, wx_l, wx_m, wx_r, out_ref, co_ref, wx_ref, tgt_ref, sem
):
    nleaf = co_m.shape[0]
    count = out_ref.shape[0]
    nvec = out_ref.shape[1]
    copies = []
    for n, (src, dst) in enumerate(
        ((co_l, co_ref), (co_m, co_ref), (co_r, co_ref), (wx_l, wx_ref), (wx_m, wx_ref), (wx_r, wx_ref))
    ):
        copies.append(
            pltpu.make_async_copy(src, dst.at[pl.ds((n % 3) * nleaf, nleaf)], sem.at[n])
        )
        copies[-1].start()
    co_ref[3 * nleaf] = jnp.zeros(co_ref.shape[1:], F32)
    wx_ref[3 * nleaf] = jnp.zeros(wx_ref.shape[1:], F32)
    for c in copies:
        c.wait()

    def target(t, carry):
        own = co_ref[list_ref[t, 29]]
        for c in range(3):
            tgt_ref[c] = jnp.broadcast_to(own[c : c + 1], (128, 128)).T

        def pair(k, acc):
            his, los, ws = [], [], []
            for s in range(2):
                m = list_ref[t, 2 * k + s]
                co = co_ref[m]
                d0 = tgt_ref[0] - co[0:1]
                d1 = tgt_ref[1] - co[1:2]
                d2 = tgt_ref[2] - co[2:3]
                kern = lax.rsqrt(d0 * d0 + d1 * d1 + (d2 * d2 + SOFT_SQ))
                hi, lo = split(kern)
                his.append(hi)
                los.append(lo)
                whi, wlo = split(wx_ref[m])
                ws.append(jnp.concatenate([whi, wlo], axis=0))
            rhs = jnp.concatenate(
                [jnp.concatenate(his, axis=1), jnp.concatenate(los, axis=1)], axis=0
            )
            return acc + dot(jnp.concatenate(ws, axis=1), rhs, NT)

        acc = lax.fori_loop(0, list_ref[t, 28], pair, jnp.zeros((2 * nvec, 256), F32))
        out_ref[t] = acc[:nvec, :128] + acc[nvec:, :128] + acc[:nvec, 128:]
        return carry

    lax.fori_loop(0, count, target, 0)


def shift_both(x, axis):
    ends = lax.axis_size(axis) - 1
    from_left = lax.ppermute(x, axis, [(i, i + 1) for i in range(ends)])
    from_right = lax.ppermute(x, axis, [(i + 1, i) for i in range(ends)])
    return from_left, from_right


def body(vectors, coords, weights, basis, transfer, coupling, far_leaf, far_parent, near_leaf):
    nleaf, rank, width = basis.shape
    nvec = vectors.shape[0]
    npar = nleaf // 8
    noff = coupling.shape[0]
    nz = lax.axis_size("vec")
    vec = lax.axis_index("vec")
    first = (lax.axis_index("leaf") - 1) * nleaf
    first_par = (lax.axis_index("leaf") - 1) * npar
    count = nleaf // nz
    nall = nvec * nz
    slots = near_leaf.shape[1]

    leaf_x = vectors.reshape(nvec, nleaf, width).transpose(1, 0, 2)
    leaf_w = (weights * (1.0 / (4.0 * math.pi))).reshape(nleaf, 1, width)
    wx = lax.all_gather(leaf_x * leaf_w, "vec", axis=1, tiled=True)
    co = jnp.pad(coords.reshape(3, nleaf, width).transpose(1, 0, 2), ((0, 0), (0, 5), (0, 0)))
    co_l, co_r = shift_both(co, "leaf")

    params = pltpu.CompilerParams(vmem_limit_bytes=VMEM_BYTES)
    coeff = pl.pallas_call(
        up_kernel,
        out_shape=jax.ShapeDtypeStruct((nleaf, nvec, rank), F32),
        compiler_params=params,
        name="up",
        cost_estimate=pl.CostEstimate(flops=10**8, bytes_accessed=4 * 10**6, transcendentals=0),
    )(leaf_x, basis)
    coeff = coeff.reshape(nleaf, nvec * rank)
    c_l, c_r = shift_both(coeff, "leaf")
    wx_l, wx_r = shift_both(wx, "leaf")

    per = 4
    rows = -(-(nleaf + npar) // 16) * 16
    idx = jnp.concatenate(
        [
            jnp.where(far_leaf >= 0, far_leaf - first, -1),
            jnp.where(far_parent >= 0, far_parent - first_par + 3 * nleaf, -1),
            jnp.full((rows - nleaf - npar, noff), -1, jnp.int32),
        ],
        axis=0,
    )
    idx = idx.reshape(rows, noff // per, per).transpose(1, 0, 2)
    depth = 256
    cols = nvec * rank
    far_out = pl.pallas_call(
        far_kernel,
        out_shape=jax.ShapeDtypeStruct((nvec, nleaf * width), F32),
        scratch_shapes=[
            pltpu.VMEM((cols // 128, depth, 128), F32),
            pltpu.VMEM((depth, 2 * cols), BF16),
            pltpu.VMEM((cols // 128, nleaf, 128), F32),
        ],
        compiler_params=params,
        name="far",
        cost_estimate=pl.CostEstimate(flops=10**10, bytes_accessed=10**8, transcendentals=0),
    )(c_l, coeff, c_r, transfer, coupling, idx, basis)

    mine = lax.dynamic_slice_in_dim(near_leaf, vec * count, count, axis=0)
    live = mine >= 0
    at = jnp.arange(slots)
    place = jnp.sum(live[:, None, :] & (at[None, None, :] < at[None, :, None]), axis=2)
    empty = 3 * nleaf
    j = jnp.arange(28)
    lists = empty + jnp.sum(
        jnp.where(
            live[:, None, :] & (place[:, None, :] == j[None, :, None]),
            (mine - first - empty)[:, None, :],
            0,
        ),
        axis=2,
    )
    pairs = (jnp.sum(live, axis=1) + 1) // 2
    own = nleaf + vec * count + jnp.arange(count)
    lists = jnp.concatenate([lists, pairs[:, None], own[:, None]], axis=1).astype(jnp.int32)
    anywhere = pl.BlockSpec(memory_space=pl.ANY)
    near = pl.pallas_call(
        near_kernel,
        out_shape=jax.ShapeDtypeStruct((count, nall, width), F32),
        in_specs=[pl.BlockSpec(memory_space=pltpu.SMEM)] + [anywhere] * 6,
        scratch_shapes=[
            pltpu.VMEM((3 * nleaf + 1, 8, width), F32),
            pltpu.VMEM((3 * nleaf + 1, nall, width), F32),
            pltpu.VMEM((3, width, width), F32),
            pltpu.SemaphoreType.DMA((6,)),
        ],
        compiler_params=params,
        name="near",
        cost_estimate=pl.CostEstimate(flops=10**10, bytes_accessed=10**8, transcendentals=0),
    )(lists, co_l, co, co_r, wx_l, wx, wx_r)
    near = lax.all_to_all(near, "vec", split_axis=1, concat_axis=0, tiled=True)
    return far_out + near.transpose(1, 0, 2).reshape(nvec, nleaf * width)


def solution(mesh):
    in_specs = (
        P("vec", ("groups", "leaf")),
        P(None, ("groups", "leaf")),
        P(("groups", "leaf")),
        P(("groups", "leaf"), None, None),
        P(),
        P(),
        P(("groups", "leaf"), None),
        P(("groups", "leaf"), None),
        P(("groups", "leaf"), None),
    )
    out_specs = P("vec", ("groups", "leaf"))
    return jax.shard_map(body, mesh=mesh, in_specs=in_specs, out_specs=out_specs, check_vma=False)
```

```python
import functools
import math

import jax
import jax.numpy as jnp
from jax import lax
from jax.experimental import pallas as pl
from jax.experimental.pallas import tpu as pltpu
from jax.sharding import PartitionSpec as P

SOFT_SQ = 0.0001
F32 = jnp.float32
BF16 = jnp.bfloat16
FAR_STEP = 32
NEAR_STEP = 4
VMEM_BYTES = 48 * 1024 * 1024
NT = (((1,), (1,)), ((), ()))
NN = (((1,), (0,)), ((), ()))


def split(x):
    hi = x.astype(BF16)
    lo = (x - hi.astype(F32)).astype(BF16)
    return hi, lo


def dot(a, b, dims):
    return lax.dot_general(a, b, dims, preferred_element_type=F32)


def dot3(a, b, dims):
    ahi, alo = split(a)
    bhi, blo = split(b)
    return dot(ahi, bhi, dims) + dot(ahi, blo, dims) + dot(alo, bhi, dims)


def twice_diag(c):
    z = jnp.zeros_like(c)
    return jnp.concatenate(
        [jnp.concatenate([c, z], axis=1), jnp.concatenate([z, c], axis=1)], axis=0
    )


def up_kernel(x_ref, basis_ref, out_ref):
    nleaf, nvec, _ = x_ref.shape
    rank = basis_ref.shape[1]

    def step(leaf, carry):
        x = x_ref[leaf]
        xhi = x.astype(BF16).astype(F32)
        lhs = jnp.concatenate([xhi, x - xhi], axis=0).astype(BF16)
        bhi, blo = split(basis_ref[leaf])
        r = dot(lhs, jnp.concatenate([bhi, blo], axis=0), NT)
        out_ref[leaf] = r[:nvec, :rank] + r[nvec:, :rank] + r[:nvec, rank:]
        return carry

    lax.fori_loop(0, nleaf, step, 0, unroll=8)


def far_kernel(
    left_ref, mid_ref, right_ref, transfer_ref, coupling_ref, leaf_ref, parent_ref, basis_ref,
    out_ref, all_ref, src_ref, loc_ref, idx_ref, wide_ref,
):
    nleaf, cols = mid_ref.shape
    nvec = out_ref.shape[0]
    rank = basis_ref.shape[1]
    npair = cols // 128
    nsrc = 3 * nleaf
    npar = nleaf // 8
    rows = idx_ref.shape[1]
    noff = coupling_ref.shape[2]
    per = FAR_STEP
    depth = src_ref.shape[0]

    def widen(r, carry):
        m = coupling_ref[r]
        wide_ref[pl.ds(r, noff, stride=rank), :] = jnp.concatenate([m, m], axis=0).T
        return carry

    lax.fori_loop(0, rank, widen, 0, unroll=4)
    spare = wide_ref.shape[0] - noff * rank
    wide_ref[noff * rank :] = jnp.zeros((spare, 128), F32)

    first = (lax.axis_index("leaf") - 1) * nleaf
    first_par = (lax.axis_index("leaf") - 1) * npar
    for b in range(-(-noff // 128)):
        at = slice(b * 128, min(noff, (b + 1) * 128))
        width = at.stop - at.start
        lists = leaf_ref[:, at]
        parents = parent_ref[:, at]
        idx_ref[b] = jnp.full((rows, 128), -1, jnp.int32)
        idx_ref[b, :nleaf, :width] = jnp.where(lists >= 0, lists - first, -1)
        idx_ref[b, nleaf : nleaf + npar, :width] = jnp.where(
            parents >= 0, parents - first_par + nsrc, -1
        )

    for p in range(npair):
        at = slice(p * 128, (p + 1) * 128)
        all_ref[p, :nleaf] = left_ref[:, at]
        all_ref[p, nleaf : 2 * nleaf] = mid_ref[:, at]
        all_ref[p, 2 * nleaf : nsrc] = right_ref[:, at]
        all_ref[p, nsrc:depth] = jnp.zeros((depth - nsrc, 128), F32)
    par = [jnp.zeros((3 * npar, 128), F32) for _ in range(npair)]
    for j in range(8):
        w = twice_diag(transfer_ref[j])
        for p in range(npair):
            c = all_ref[p, pl.ds(j, 3 * npar, stride=8), :]
            par[p] = par[p] + dot3(c, w, NT)
    for p in range(npair):
        all_ref[p, nsrc : nsrc + 3 * npar] = par[p]
        hi, lo = split(all_ref[p])
        src_ref[:, p * 128 : (p + 1) * 128] = hi
        src_ref[:, cols + p * 128 : cols + (p + 1) * 128] = lo

    lane = lax.broadcasted_iota(jnp.int32, (rows, depth), 1)
    low = lax.broadcasted_iota(jnp.int32, (1, 128), 1) < rank

    def block_pair(o):
        c = [wide_ref[pl.ds(pl.multiple_of((o + k) * rank, rank), rank), :] for k in range(2)]
        return split(jnp.where(low, c[0], c[1]))

    def couple(b, i, acc):
        idx = pltpu.roll(idx_ref[b], (128 - per * i) % 128, 1)
        hot = [
            jnp.where(idx[:, j : j + 1] == lane, 1.0, 0.0).astype(BF16) for j in range(per)
        ]
        got = dot(jnp.concatenate(hot, axis=0), src_ref[...], NN).astype(BF16)
        w = [block_pair(b * 128 + i * per + j) for j in range(0, per, 2)]
        w = [jnp.concatenate([x[n] for x in w], axis=1) for n in range(2)]
        lhs = []
        for p in range(2 * npair):
            for v in range(2):
                at = slice(p * 128 + v * rank, p * 128 + (v + 1) * rank)
                lhs.append(
                    jnp.concatenate(
                        [got[j * rows : (j + 1) * rows, at] for j in range(per)], axis=1
                    )
                )
        return acc + dot(jnp.concatenate(lhs, axis=0), jnp.concatenate(w, axis=0), NT)

    acc = jnp.zeros((2 * nvec * rows, 2 * rank), F32)
    for b in range(-(-noff // 128)):
        steps = -(-min(128, noff - b * 128) // per)
        acc = lax.fori_loop(0, steps, functools.partial(couple, b), acc, unroll=1)
    hi_part, lo_part = acc[: nvec * rows], acc[nvec * rows :]
    total = hi_part[:, :rank] + hi_part[:, rank:] + lo_part[:, :rank]
    total = jnp.concatenate(
        [
            jnp.concatenate(
                [total[v * rows : (v + 1) * rows] for v in (2 * p, 2 * p + 1)], axis=1
            )
            for p in range(npair)
        ],
        axis=0,
    )
    for p in range(npair):
        loc_ref[p] = total[p * rows : p * rows + nleaf]
    for j in range(8):
        w = twice_diag(transfer_ref[j])
        for p in range(npair):
            far = 0.5 * total[p * rows + nleaf : p * rows + nleaf + npar]
            at = (p, pl.ds(j, npar, stride=8), slice(None))
            loc_ref[at] = loc_ref[at] + dot3(far, w, NN)

    def leaf_out(leaf, carry):
        parts = []
        for p in range(npair):
            piece = loc_ref[p, pl.ds(leaf, 1), :]
            parts.append(jnp.where(low, piece, 0.0))
            parts.append(jnp.where(low, 0.0, piece))
        lhs = jnp.concatenate(parts, axis=0)
        lhi = lhs.astype(BF16).astype(F32)
        lhs = jnp.concatenate([lhi, lhs - lhi], axis=0).astype(BF16)
        bhi, blo = split(basis_ref[leaf])
        b = jnp.concatenate([bhi, blo], axis=1)
        r = dot(lhs, jnp.concatenate([b, b], axis=0), NN)
        out_ref[:, pl.ds(pl.multiple_of(leaf * 128, 128), 128)] = (
            r[:nvec, :128] + r[nvec:, :128] + r[:nvec, 128:]
        )
        return carry

    lax.fori_loop(0, nleaf, leaf_out, 0, unroll=8)


def near_kernel(
    list_ref, co_l, co_m, co_r, wx_l, wx_m, wx_r, out_ref, co_ref, wx_ref, tgt_ref, sem
):
    nleaf = co_m.shape[0]
    nz, count, nvec = out_ref.shape[:3]
    nall = nz * nvec
    own_at = list_ref.shape[1] - 1 - nz
    copies = []
    for n, (src, dst) in enumerate(
        ((co_l, co_ref), (co_m, co_ref), (co_r, co_ref), (wx_l, wx_ref), (wx_m, wx_ref), (wx_r, wx_ref))
    ):
        copies.append(
            pltpu.make_async_copy(src, dst.at[pl.ds((n % 3) * nleaf, nleaf)], sem.at[n])
        )
        copies[-1].start()
    co_ref[3 * nleaf] = jnp.zeros(co_ref.shape[1:], F32)
    wx_ref[3 * nleaf] = jnp.zeros(wx_ref.shape[1:], F32)
    for c in copies:
        c.wait()

    def target(t, carry):
        own = jnp.transpose(co_ref[list_ref[t, own_at]])
        for c in range(3):
            tgt_ref[c] = jnp.broadcast_to(own[:, c : c + 1], (128, 128))

        def step(k, acc):
            for g in range(NEAR_STEP):
                his, los, ws = [], [], []
                for s in range(2):
                    m = list_ref[t, 2 * (k * NEAR_STEP + g) + s]
                    co = co_ref[m]
                    d0 = tgt_ref[0] - co[0:1]
                    d1 = tgt_ref[1] - co[1:2]
                    d2 = tgt_ref[2] - co[2:3]
                    kern = lax.rsqrt(d0 * d0 + d1 * d1 + (d2 * d2 + SOFT_SQ))
                    hi, lo = split(kern)
                    his.append(hi)
                    los.append(lo)
                    whi, wlo = split(wx_ref[m])
                    ws.append(jnp.concatenate([whi, wlo], axis=0))
                rhs = jnp.concatenate(
                    [jnp.concatenate(his, axis=1), jnp.concatenate(los, axis=1)], axis=0
                )
                acc = acc + dot(jnp.concatenate(ws, axis=1), rhs, NT)
            return acc

        acc = lax.fori_loop(0, list_ref[t, own_at - 1], step, jnp.zeros((2 * nall, 256), F32))
        x = acc[:nall, :128] + acc[nall:, :128] + acc[:nall, 128:]
        for k in range(nz):
            out_ref[list_ref[t, own_at + 1 + k], t] = x[k * nvec : (k + 1) * nvec]
        return carry

    lax.fori_loop(0, count, target, 0)


def shift_both(x, axis):
    ends = lax.axis_size(axis) - 1
    from_left = lax.ppermute(x, axis, [(i, i + 1) for i in range(ends)])
    from_right = lax.ppermute(x, axis, [(i + 1, i) for i in range(ends)])
    return from_left, from_right


def body(vectors, coords, weights, basis, transfer, coupling, far_leaf, far_parent, near_leaf):
    nleaf, rank, width = basis.shape
    nvec = vectors.shape[0]
    npar = nleaf // 8
    noff = coupling.shape[0]
    nz = lax.axis_size("vec")
    vec = lax.axis_index("vec")
    first = (lax.axis_index("leaf") - 1) * nleaf
    first_par = (lax.axis_index("leaf") - 1) * npar
    count = nleaf // nz
    nall = nvec * nz
    slots = near_leaf.shape[1]

    leaf_x = vectors.reshape(nvec, nleaf, width).transpose(1, 0, 2)
    leaf_w = (weights * (1.0 / (4.0 * math.pi))).reshape(nleaf, 1, width)
    piece = leaf_x * leaf_w
    pieces = [piece] + [
        lax.ppermute(piece, "vec", [(i, (i + k) % nz) for i in range(nz)]) for k in range(1, nz)
    ]
    wx = jnp.concatenate(pieces, axis=1)
    co = jnp.pad(coords.reshape(3, nleaf, width).transpose(1, 0, 2), ((0, 0), (0, 5), (0, 0)))
    co_l, co_r = shift_both(co, "leaf")

    params = pltpu.CompilerParams(vmem_limit_bytes=VMEM_BYTES)
    coeff = pl.pallas_call(
        up_kernel,
        out_shape=jax.ShapeDtypeStruct((nleaf, nvec, rank), F32),
        compiler_params=params,
        name="up",
        cost_estimate=pl.CostEstimate(flops=10**8, bytes_accessed=4 * 10**6, transcendentals=0),
    )(leaf_x, basis)
    coeff = coeff.reshape(nleaf, nvec * rank)
    c_l, c_r = shift_both(coeff, "leaf")
    wx_l, wx_r = shift_both(wx, "leaf")

    rows = -(-(nleaf + npar) // 16) * 16
    padded = -(-noff // FAR_STEP) * FAR_STEP
    depth = 256
    cols = nvec * rank
    far_out = pl.pallas_call(
        far_kernel,
        out_shape=jax.ShapeDtypeStruct((nvec, nleaf * width), F32),
        scratch_shapes=[
            pltpu.VMEM((cols // 128, depth, 128), F32),
            pltpu.VMEM((depth, 2 * cols), BF16),
            pltpu.VMEM((cols // 128, nleaf, 128), F32),
            pltpu.VMEM((-(-noff // 128), rows, 128), jnp.int32),
            pltpu.VMEM((padded * rank, 128), F32),
        ],
        compiler_params=params,
        name="far",
        cost_estimate=pl.CostEstimate(flops=10**10, bytes_accessed=10**8, transcendentals=0),
    )(c_l, coeff, c_r, transfer, coupling.transpose(1, 2, 0), far_leaf, far_parent, basis)

    mine = lax.dynamic_slice_in_dim(near_leaf, vec * count, count, axis=0)
    live = mine >= 0
    at = jnp.arange(slots)
    place = jnp.sum(live[:, None, :] & (at[None, None, :] < at[None, :, None]), axis=2)
    empty = 3 * nleaf
    group = 2 * NEAR_STEP
    j = jnp.arange(-(-slots // group) * group)
    lists = empty + jnp.sum(
        jnp.where(
            live[:, None, :] & (place[:, None, :] == j[None, :, None]),
            (mine - first - empty)[:, None, :],
            0,
        ),
        axis=2,
    )
    steps = (jnp.sum(live, axis=1) + group - 1) // group
    own = nleaf + vec * count + jnp.arange(count)
    lists = jnp.concatenate(
        [lists, steps[:, None], own[:, None], jnp.broadcast_to((vec - jnp.arange(nz)) % nz, (count, nz))],
        axis=1,
    ).astype(jnp.int32)
    anywhere = pl.BlockSpec(memory_space=pl.ANY)
    near = pl.pallas_call(
        near_kernel,
        out_shape=jax.ShapeDtypeStruct((nz, count, nvec, width), F32),
        in_specs=[pl.BlockSpec(memory_space=pltpu.SMEM)] + [anywhere] * 6,
        scratch_shapes=[
            pltpu.VMEM((3 * nleaf + 1, 8, width), F32),
            pltpu.VMEM((3 * nleaf + 1, nall, width), F32),
            pltpu.VMEM((3, width, width), F32),
            pltpu.SemaphoreType.DMA((6,)),
        ],
        compiler_params=params,
        name="near",
        cost_estimate=pl.CostEstimate(flops=10**10, bytes_accessed=10**8, transcendentals=0),
    )(lists, co_l, co, co_r, wx_l, wx, wx_r)
    near = lax.all_to_all(near, "vec", split_axis=0, concat_axis=0, tiled=True)
    near = near.reshape(nleaf, nvec, width)
    return far_out + near.transpose(1, 0, 2).reshape(nvec, nleaf * width)


def solution(mesh):
    in_specs = (
        P("vec", ("groups", "leaf")),
        P(None, ("groups", "leaf")),
        P(("groups", "leaf")),
        P(("groups", "leaf"), None, None),
        P(),
        P(),
        P(("groups", "leaf"), None),
        P(("groups", "leaf"), None),
        P(("groups", "leaf"), None),
    )
    out_specs = P("vec", ("groups", "leaf"))
    return jax.shard_map(body, mesh=mesh, in_specs=in_specs, out_specs=out_specs, check_vma=False)
```

```python
import functools
import math

import jax
import jax.numpy as jnp
from jax import lax
from jax.experimental import pallas as pl
from jax.experimental.pallas import tpu as pltpu
from jax.sharding import PartitionSpec as P

SOFT_SQ = 0.0001
F32 = jnp.float32
BF16 = jnp.bfloat16
FAR_STEP = 32
NEAR_STEP = 4
VMEM_BYTES = 48 * 1024 * 1024
NT = (((1,), (1,)), ((), ()))
NN = (((1,), (0,)), ((), ()))


def split(x):
    hi = x.astype(BF16)
    lo = (x - hi.astype(F32)).astype(BF16)
    return hi, lo


def dot(a, b, dims):
    return lax.dot_general(a, b, dims, preferred_element_type=F32)


def dot3(a, b, dims):
    ahi, alo = split(a)
    bhi, blo = split(b)
    return dot(ahi, bhi, dims) + dot(ahi, blo, dims) + dot(alo, bhi, dims)


def twice_diag(c):
    z = jnp.zeros_like(c)
    return jnp.concatenate(
        [jnp.concatenate([c, z], axis=1), jnp.concatenate([z, c], axis=1)], axis=0
    )


def link_kernel(
    x_ref, w_ref, co_ref, basis_ref,
    wx_ref, co_l, co_r, c_l, c_m, c_r,
    piece, own, send_sem, recv_sem, copy_sem,
):
    nleaf, nvec, _ = x_ref.shape
    rank = basis_ref.shape[1]
    nz = wx_ref.shape[0]
    nl = lax.axis_size("leaf")
    vec, leaf_at = lax.axis_index("vec"), lax.axis_index("leaf")
    right, left = lax.rem(leaf_at + 1, nl), lax.rem(leaf_at + nl - 1, nl)
    peers = [{"vec": lax.rem(vec + k, nz)} for k in range(1, nz)]
    mesh_id = pl.DeviceIdType.MESH

    barrier = pltpu.get_barrier_semaphore()
    for who in peers + [{"leaf": right}, {"leaf": left}]:
        pl.semaphore_signal(barrier, inc=1, device_id=who, device_id_type=mesh_id)
    piece[...] = x_ref[...] * w_ref[...]
    pl.semaphore_wait(barrier, nz + 1)

    def send(n, src, dst, who):
        copy = pltpu.make_async_remote_copy(
            src_ref=src, dst_ref=dst, send_sem=send_sem.at[n], recv_sem=recv_sem.at[n],
            device_id=who, device_id_type=mesh_id,
        )
        copy.start()
        return copy

    sent = [send(n, piece, wx_ref.at[vec], who) for n, who in enumerate(peers)]
    sent.append(send(nz - 1, co_ref, co_l, {"leaf": right}))
    sent.append(send(nz, co_ref, co_r, {"leaf": left}))
    keep = pltpu.make_async_copy(piece, wx_ref.at[vec], copy_sem.at[0])
    keep.start()

    def step(leaf, carry):
        x = x_ref[leaf]
        xhi = x.astype(BF16).astype(F32)
        lhs = jnp.concatenate([xhi, x - xhi], axis=0).astype(BF16)
        bhi, blo = split(basis_ref[leaf])
        r = dot(lhs, jnp.concatenate([bhi, blo], axis=0), NT)
        c = r[:nvec, :rank] + r[nvec:, :rank] + r[:nvec, rank:]
        own[pl.ds(leaf, 1), :] = jnp.concatenate([c[v : v + 1] for v in range(nvec)], axis=1)
        return carry

    lax.fori_loop(0, nleaf, step, 0, unroll=8)
    sent.append(send(nz + 1, own, c_l, {"leaf": right}))
    sent.append(send(nz + 2, own, c_r, {"leaf": left}))
    keep_c = pltpu.make_async_copy(own, c_m, copy_sem.at[1])
    keep_c.start()
    for copy in sent:
        copy.wait()
    keep.wait()
    keep_c.wait()


def far_kernel(
    left_ref, mid_ref, right_ref, transfer_ref, coupling_ref, leaf_ref, parent_ref, basis_ref,
    out_ref, all_ref, src_ref, loc_ref, idx_ref, wide_ref,
):
    nleaf, cols = mid_ref.shape
    nvec = out_ref.shape[0]
    rank = basis_ref.shape[1]
    npair = cols // 128
    nsrc = 3 * nleaf
    npar = nleaf // 8
    rows = idx_ref.shape[1]
    noff = coupling_ref.shape[2]
    per = FAR_STEP
    depth = src_ref.shape[0]

    def widen(r, carry):
        m = coupling_ref[r]
        wide_ref[pl.ds(r, noff, stride=rank), :] = jnp.concatenate([m, m], axis=0).T
        return carry

    lax.fori_loop(0, rank, widen, 0, unroll=4)
    spare = wide_ref.shape[0] - noff * rank
    wide_ref[noff * rank :] = jnp.zeros((spare, 128), F32)

    first = (lax.axis_index("leaf") - 1) * nleaf
    first_par = (lax.axis_index("leaf") - 1) * npar
    for b in range(-(-noff // 128)):
        at = slice(b * 128, min(noff, (b + 1) * 128))
        width = at.stop - at.start
        lists = leaf_ref[:, at]
        parents = parent_ref[:, at]
        idx_ref[b] = jnp.full((rows, 128), -1, jnp.int32)
        idx_ref[b, :nleaf, :width] = jnp.where(lists >= 0, lists - first, -1)
        idx_ref[b, nleaf : nleaf + npar, :width] = jnp.where(
            parents >= 0, parents - first_par + nsrc, -1
        )

    for p in range(npair):
        at = slice(p * 128, (p + 1) * 128)
        all_ref[p, :nleaf] = left_ref[:, at]
        all_ref[p, nleaf : 2 * nleaf] = mid_ref[:, at]
        all_ref[p, 2 * nleaf : nsrc] = right_ref[:, at]
        all_ref[p, nsrc:depth] = jnp.zeros((depth - nsrc, 128), F32)
    par = [jnp.zeros((3 * npar, 128), F32) for _ in range(npair)]
    for j in range(8):
        w = twice_diag(transfer_ref[j])
        for p in range(npair):
            c = all_ref[p, pl.ds(j, 3 * npar, stride=8), :]
            par[p] = par[p] + dot3(c, w, NT)
    for p in range(npair):
        all_ref[p, nsrc : nsrc + 3 * npar] = par[p]
        hi, lo = split(all_ref[p])
        src_ref[:, p * 128 : (p + 1) * 128] = hi
        src_ref[:, cols + p * 128 : cols + (p + 1) * 128] = lo

    lane = lax.broadcasted_iota(jnp.int32, (rows, depth), 1)
    low = lax.broadcasted_iota(jnp.int32, (1, 128), 1) < rank

    def block_pair(o):
        c = [wide_ref[pl.ds(pl.multiple_of((o + k) * rank, rank), rank), :] for k in range(2)]
        return split(jnp.where(low, c[0], c[1]))

    def couple(b, i, acc):
        idx = pltpu.roll(idx_ref[b], (128 - per * i) % 128, 1)
        hot = [
            jnp.where(idx[:, j : j + 1] == lane, 1.0, 0.0).astype(BF16) for j in range(per)
        ]
        got = dot(jnp.concatenate(hot, axis=0), src_ref[...], NN).astype(BF16)
        w = [block_pair(b * 128 + i * per + j) for j in range(0, per, 2)]
        w = [jnp.concatenate([x[n] for x in w], axis=1) for n in range(2)]
        lhs = []
        for p in range(2 * npair):
            for v in range(2):
                at = slice(p * 128 + v * rank, p * 128 + (v + 1) * rank)
                lhs.append(
                    jnp.concatenate(
                        [got[j * rows : (j + 1) * rows, at] for j in range(per)], axis=1
                    )
                )
        return acc + dot(jnp.concatenate(lhs, axis=0), jnp.concatenate(w, axis=0), NT)

    acc = jnp.zeros((2 * nvec * rows, 2 * rank), F32)
    for b in range(-(-noff // 128)):
        steps = -(-min(128, noff - b * 128) // per)
        acc = lax.fori_loop(0, steps, functools.partial(couple, b), acc, unroll=1)
    hi_part, lo_part = acc[: nvec * rows], acc[nvec * rows :]
    total = hi_part[:, :rank] + hi_part[:, rank:] + lo_part[:, :rank]
    total = jnp.concatenate(
        [
            jnp.concatenate(
                [total[v * rows : (v + 1) * rows] for v in (2 * p, 2 * p + 1)], axis=1
            )
            for p in range(npair)
        ],
        axis=0,
    )
    for p in range(npair):
        loc_ref[p] = total[p * rows : p * rows + nleaf]
    for j in range(8):
        w = twice_diag(transfer_ref[j])
        for p in range(npair):
            far = 0.5 * total[p * rows + nleaf : p * rows + nleaf + npar]
            at = (p, pl.ds(j, npar, stride=8), slice(None))
            loc_ref[at] = loc_ref[at] + dot3(far, w, NN)

    def leaf_out(leaf, carry):
        parts = []
        for p in range(npair):
            piece = loc_ref[p, pl.ds(leaf, 1), :]
            parts.append(jnp.where(low, piece, 0.0))
            parts.append(jnp.where(low, 0.0, piece))
        lhs = jnp.concatenate(parts, axis=0)
        lhi = lhs.astype(BF16).astype(F32)
        lhs = jnp.concatenate([lhi, lhs - lhi], axis=0).astype(BF16)
        bhi, blo = split(basis_ref[leaf])
        b = jnp.concatenate([bhi, blo], axis=1)
        r = dot(lhs, jnp.concatenate([b, b], axis=0), NN)
        out_ref[:, pl.ds(pl.multiple_of(leaf * 128, 128), 128)] = (
            r[:nvec, :128] + r[nvec:, :128] + r[:nvec, 128:]
        )
        return carry

    lax.fori_loop(0, nleaf, leaf_out, 0, unroll=8)


def near_kernel(
    list_ref, co_l, co_m, co_r, wx_l, wx_m, wx_r, out_ref, co_ref, wx_ref, tgt_ref, sem
):
    nleaf = co_m.shape[0]
    nz, count, nvec = out_ref.shape[:3]
    nall = nz * nvec
    own_at = list_ref.shape[1] - 1 - nz
    copies = []
    for n, (src, dst) in enumerate(
        ((co_l, co_ref), (co_m, co_ref), (co_r, co_ref), (wx_l, wx_ref), (wx_m, wx_ref), (wx_r, wx_ref))
    ):
        copies.append(
            pltpu.make_async_copy(src, dst.at[pl.ds((n % 3) * nleaf, nleaf)], sem.at[n])
        )
        copies[-1].start()
    co_ref[3 * nleaf] = jnp.zeros(co_ref.shape[1:], F32)
    wx_ref[3 * nleaf] = jnp.zeros(wx_ref.shape[1:], F32)
    for c in copies:
        c.wait()

    def target(t, carry):
        own = jnp.transpose(co_ref[list_ref[t, own_at]])
        for c in range(3):
            tgt_ref[c] = jnp.broadcast_to(own[:, c : c + 1], (128, 128))

        def step(k, acc):
            for g in range(NEAR_STEP):
                his, los, ws = [], [], []
                for s in range(2):
                    m = list_ref[t, 2 * (k * NEAR_STEP + g) + s]
                    co = co_ref[m]
                    d0 = tgt_ref[0] - co[0:1]
                    d1 = tgt_ref[1] - co[1:2]
                    d2 = tgt_ref[2] - co[2:3]
                    kern = lax.rsqrt(d0 * d0 + d1 * d1 + (d2 * d2 + SOFT_SQ))
                    hi, lo = split(kern)
                    his.append(hi)
                    los.append(lo)
                    whi, wlo = split(wx_ref[m])
                    ws.append(jnp.concatenate([whi, wlo], axis=0))
                rhs = jnp.concatenate(
                    [jnp.concatenate(his, axis=1), jnp.concatenate(los, axis=1)], axis=0
                )
                acc = acc + dot(jnp.concatenate(ws, axis=1), rhs, NT)
            return acc

        acc = lax.fori_loop(0, list_ref[t, own_at - 1], step, jnp.zeros((2 * nall, 256), F32))
        x = acc[:nall, :128] + acc[nall:, :128] + acc[:nall, 128:]
        for k in range(nz):
            out_ref[list_ref[t, own_at + 1 + k], t] = x[k * nvec : (k + 1) * nvec]
        return carry

    lax.fori_loop(0, count, target, 0)


def shift_both(x, axis):
    ends = lax.axis_size(axis) - 1
    from_left = lax.ppermute(x, axis, [(i, i + 1) for i in range(ends)])
    from_right = lax.ppermute(x, axis, [(i + 1, i) for i in range(ends)])
    return from_left, from_right


def body(vectors, coords, weights, basis, transfer, coupling, far_leaf, far_parent, near_leaf):
    nleaf, rank, width = basis.shape
    nvec = vectors.shape[0]
    npar = nleaf // 8
    noff = coupling.shape[0]
    nz = lax.axis_size("vec")
    vec = lax.axis_index("vec")
    first = (lax.axis_index("leaf") - 1) * nleaf
    first_par = (lax.axis_index("leaf") - 1) * npar
    count = nleaf // nz
    nall = nvec * nz
    slots = near_leaf.shape[1]

    leaf_x = vectors.reshape(nvec, nleaf, width).transpose(1, 0, 2)
    leaf_w = (weights * (1.0 / (4.0 * math.pi))).reshape(nleaf, 1, width)
    co = jnp.pad(coords.reshape(3, nleaf, width).transpose(1, 0, 2), ((0, 0), (0, 5), (0, 0)))
    params = pltpu.CompilerParams(vmem_limit_bytes=VMEM_BYTES)
    cols = nvec * rank
    in_vmem = pl.BlockSpec(memory_space=pltpu.VMEM)
    anywhere = pl.BlockSpec(memory_space=pl.ANY)
    side = jax.ShapeDtypeStruct((nleaf, cols), F32)
    co_side = jax.ShapeDtypeStruct(co.shape, F32)
    wx, co_l, co_r, c_l, coeff, c_r = pl.pallas_call(
        link_kernel,
        out_shape=(
            jax.ShapeDtypeStruct((nz, nleaf, nvec, width), F32), co_side, co_side, side, side, side,
        ),
        in_specs=[in_vmem] * 4,
        out_specs=(anywhere,) * 6,
        scratch_shapes=[
            pltpu.VMEM((nleaf, nvec, width), F32),
            pltpu.VMEM((nleaf, cols), F32),
            pltpu.SemaphoreType.DMA((nz + 3,)),
            pltpu.SemaphoreType.DMA((nz + 3,)),
            pltpu.SemaphoreType.DMA((2,)),
        ],
        compiler_params=pltpu.CompilerParams(
            vmem_limit_bytes=VMEM_BYTES, collective_id=0, has_side_effects=True
        ),
        name="link",
        cost_estimate=pl.CostEstimate(flops=10**8, bytes_accessed=4 * 10**6, transcendentals=0),
    )(leaf_x, leaf_w, co, basis)
    wx = wx.transpose(1, 0, 2, 3).reshape(nleaf, nz * nvec, width)
    wx_l, wx_r = shift_both(wx, "leaf")

    rows = -(-(nleaf + npar) // 16) * 16
    padded = -(-noff // FAR_STEP) * FAR_STEP
    depth = 256
    far_out = pl.pallas_call(
        far_kernel,
        out_shape=jax.ShapeDtypeStruct((nvec, nleaf * width), F32),
        scratch_shapes=[
            pltpu.VMEM((cols // 128, depth, 128), F32),
            pltpu.VMEM((depth, 2 * cols), BF16),
            pltpu.VMEM((cols // 128, nleaf, 128), F32),
            pltpu.VMEM((-(-noff // 128), rows, 128), jnp.int32),
            pltpu.VMEM((padded * rank, 128), F32),
        ],
        compiler_params=params,
        name="far",
        cost_estimate=pl.CostEstimate(flops=10**10, bytes_accessed=10**8, transcendentals=0),
    )(c_l, coeff, c_r, transfer, coupling.transpose(1, 2, 0), far_leaf, far_parent, basis)

    mine = lax.dynamic_slice_in_dim(near_leaf, vec * count, count, axis=0)
    live = mine >= 0
    at = jnp.arange(slots)
    place = jnp.sum(live[:, None, :] & (at[None, None, :] < at[None, :, None]), axis=2)
    empty = 3 * nleaf
    group = 2 * NEAR_STEP
    j = jnp.arange(-(-slots // group) * group)
    lists = empty + jnp.sum(
        jnp.where(
            live[:, None, :] & (place[:, None, :] == j[None, :, None]),
            (mine - first - empty)[:, None, :],
            0,
        ),
        axis=2,
    )
    steps = (jnp.sum(live, axis=1) + group - 1) // group
    own = nleaf + vec * count + jnp.arange(count)
    lists = jnp.concatenate(
        [lists, steps[:, None], own[:, None], jnp.broadcast_to(jnp.arange(nz), (count, nz))],
        axis=1,
    ).astype(jnp.int32)
    near = pl.pallas_call(
        near_kernel,
        out_shape=jax.ShapeDtypeStruct((nz, count, nvec, width), F32),
        in_specs=[pl.BlockSpec(memory_space=pltpu.SMEM)] + [anywhere] * 6,
        scratch_shapes=[
            pltpu.VMEM((3 * nleaf + 1, 8, width), F32),
            pltpu.VMEM((3 * nleaf + 1, nall, width), F32),
            pltpu.VMEM((3, width, width), F32),
            pltpu.SemaphoreType.DMA((6,)),
        ],
        compiler_params=params,
        name="near",
        cost_estimate=pl.CostEstimate(flops=10**10, bytes_accessed=10**8, transcendentals=0),
    )(lists, co_l, co, co_r, wx_l, wx, wx_r)
    near = lax.all_to_all(near, "vec", split_axis=0, concat_axis=0, tiled=True)
    near = near.reshape(nleaf, nvec, width)
    return far_out + near.transpose(1, 0, 2).reshape(nvec, nleaf * width)


def solution(mesh):
    in_specs = (
        P("vec", ("groups", "leaf")),
        P(None, ("groups", "leaf")),
        P(("groups", "leaf")),
        P(("groups", "leaf"), None, None),
        P(),
        P(),
        P(("groups", "leaf"), None),
        P(("groups", "leaf"), None),
        P(("groups", "leaf"), None),
    )
    out_specs = P("vec", ("groups", "leaf"))
    return jax.shard_map(body, mesh=mesh, in_specs=in_specs, out_specs=out_specs, check_vma=False)
```

```python
import functools
import math

import jax
import jax.numpy as jnp
from jax import lax
from jax.experimental import pallas as pl
from jax.experimental.pallas import tpu as pltpu
from jax.sharding import PartitionSpec as P

SOFT_SQ = 0.0001
F32 = jnp.float32
BF16 = jnp.bfloat16
FAR_STEP = 64
NEAR_STEP = 7
VMEM_BYTES = 48 * 1024 * 1024
NT = (((1,), (1,)), ((), ()))
NN = (((1,), (0,)), ((), ()))


def split(x):
    hi = x.astype(BF16)
    lo = (x - hi.astype(F32)).astype(BF16)
    return hi, lo


def dot(a, b, dims):
    return lax.dot_general(a, b, dims, preferred_element_type=F32)


def dot3(a, b, dims):
    ahi, alo = split(a)
    bhi, blo = split(b)
    return dot(ahi, bhi, dims) + dot(ahi, blo, dims) + dot(alo, bhi, dims)


def twice_diag(c):
    z = jnp.zeros_like(c)
    return jnp.concatenate(
        [jnp.concatenate([c, z], axis=1), jnp.concatenate([z, c], axis=1)], axis=0
    )


def up_kernel(x_ref, basis_ref, out_ref):
    nleaf, nvec, _ = x_ref.shape
    rank = basis_ref.shape[1]

    def step(leaf, carry):
        x = x_ref[leaf]
        xhi = x.astype(BF16).astype(F32)
        lhs = jnp.concatenate([xhi, x - xhi], axis=0).astype(BF16)
        bhi, blo = split(basis_ref[leaf])
        r = dot(lhs, jnp.concatenate([bhi, blo], axis=0), NT)
        out_ref[leaf] = r[:nvec, :rank] + r[nvec:, :rank] + r[:nvec, rank:]
        return carry

    lax.fori_loop(0, nleaf, step, 0, unroll=8)


def far_kernel(
    left_ref, mid_ref, right_ref, transfer_ref, coupling_ref, leaf_ref, parent_ref, basis_ref,
    out_ref, all_ref, src_ref, loc_ref, idx_ref, wide_ref,
):
    nleaf, cols = mid_ref.shape
    nvec = out_ref.shape[0]
    rank = basis_ref.shape[1]
    npair = cols // 128
    nsrc = 3 * nleaf
    npar = nleaf // 8
    rows = idx_ref.shape[1]
    noff = coupling_ref.shape[2]
    per = FAR_STEP
    depth = src_ref.shape[0]

    def widen(r, carry):
        m = coupling_ref[r]
        wide_ref[pl.ds(r, noff, stride=rank), :] = jnp.concatenate([m, m], axis=0).T
        return carry

    lax.fori_loop(0, rank, widen, 0, unroll=4)
    spare = wide_ref.shape[0] - noff * rank
    wide_ref[noff * rank :] = jnp.zeros((spare, 128), F32)

    first = (lax.axis_index("leaf") - 1) * nleaf
    first_par = (lax.axis_index("leaf") - 1) * npar
    for b in range(-(-noff // 128)):
        at = slice(b * 128, min(noff, (b + 1) * 128))
        width = at.stop - at.start
        lists = leaf_ref[:, at]
        parents = parent_ref[:, at]
        idx_ref[b] = jnp.full((rows, 128), -1, jnp.int32)
        idx_ref[b, :nleaf, :width] = jnp.where(lists >= 0, lists - first, -1)
        idx_ref[b, nleaf : nleaf + npar, :width] = jnp.where(
            parents >= 0, parents - first_par + nsrc, -1
        )

    for p in range(npair):
        at = slice(p * 128, (p + 1) * 128)
        all_ref[p, :nleaf] = left_ref[:, at]
        all_ref[p, nleaf : 2 * nleaf] = mid_ref[:, at]
        all_ref[p, 2 * nleaf : nsrc] = right_ref[:, at]
        all_ref[p, nsrc:depth] = jnp.zeros((depth - nsrc, 128), F32)
    par = [jnp.zeros((3 * npar, 128), F32) for _ in range(npair)]
    for j in range(8):
        w = twice_diag(transfer_ref[j])
        for p in range(npair):
            c = all_ref[p, pl.ds(j, 3 * npar, stride=8), :]
            par[p] = par[p] + dot3(c, w, NT)
    for p in range(npair):
        all_ref[p, nsrc : nsrc + 3 * npar] = par[p]
        hi, lo = split(all_ref[p])
        src_ref[:, p * 128 : (p + 1) * 128] = hi
        src_ref[:, cols + p * 128 : cols + (p + 1) * 128] = lo

    lane = lax.broadcasted_iota(jnp.int32, (rows, depth), 1)
    low = lax.broadcasted_iota(jnp.int32, (1, 128), 1) < rank

    def block_pair(o):
        c = [wide_ref[pl.ds(pl.multiple_of((o + k) * rank, rank), rank), :] for k in range(2)]
        return split(jnp.where(low, c[0], c[1]))

    def couple(b, i, acc):
        idx = pltpu.roll(idx_ref[b], (128 - per * i) % 128, 1)
        hot = [
            jnp.where(idx[:, j : j + 1] == lane, 1.0, 0.0).astype(BF16) for j in range(per)
        ]
        got = dot(jnp.concatenate(hot, axis=0), src_ref[...], NN).astype(BF16)
        w = [block_pair(b * 128 + i * per + j) for j in range(0, per, 2)]
        w = [jnp.concatenate([x[n] for x in w], axis=1) for n in range(2)]
        lhs = []
        for p in range(2 * npair):
            for v in range(2):
                at = slice(p * 128 + v * rank, p * 128 + (v + 1) * rank)
                lhs.append(
                    jnp.concatenate(
                        [got[j * rows : (j + 1) * rows, at] for j in range(per)], axis=1
                    )
                )
        return acc + dot(jnp.concatenate(lhs, axis=0), jnp.concatenate(w, axis=0), NT)

    acc = jnp.zeros((2 * nvec * rows, 2 * rank), F32)
    for b in range(-(-noff // 128)):
        steps = -(-min(128, noff - b * 128) // per)
        acc = lax.fori_loop(0, steps, functools.partial(couple, b), acc, unroll=1)
    hi_part, lo_part = acc[: nvec * rows], acc[nvec * rows :]
    total = hi_part[:, :rank] + hi_part[:, rank:] + lo_part[:, :rank]
    total = jnp.concatenate(
        [
            jnp.concatenate(
                [total[v * rows : (v + 1) * rows] for v in (2 * p, 2 * p + 1)], axis=1
            )
            for p in range(npair)
        ],
        axis=0,
    )
    for p in range(npair):
        loc_ref[p] = total[p * rows : p * rows + nleaf]
    for j in range(8):
        w = twice_diag(transfer_ref[j])
        for p in range(npair):
            far = 0.5 * total[p * rows + nleaf : p * rows + nleaf + npar]
            at = (p, pl.ds(j, npar, stride=8), slice(None))
            loc_ref[at] = loc_ref[at] + dot3(far, w, NN)

    def leaf_out(leaf, carry):
        parts = []
        for p in range(npair):
            piece = loc_ref[p, pl.ds(leaf, 1), :]
            parts.append(jnp.where(low, piece, 0.0))
            parts.append(jnp.where(low, 0.0, piece))
        lhs = jnp.concatenate(parts, axis=0)
        lhi = lhs.astype(BF16).astype(F32)
        lhs = jnp.concatenate([lhi, lhs - lhi], axis=0).astype(BF16)
        bhi, blo = split(basis_ref[leaf])
        b = jnp.concatenate([bhi, blo], axis=1)
        r = dot(lhs, jnp.concatenate([b, b], axis=0), NN)
        out_ref[:, pl.ds(pl.multiple_of(leaf * 128, 128), 128)] = (
            r[:nvec, :128] + r[nvec:, :128] + r[:nvec, 128:]
        )
        return carry

    lax.fori_loop(0, nleaf, leaf_out, 0, unroll=8)


def near_kernel(
    list_ref, co_l, co_m, co_r, wx_l, wx_m, wx_r, out_ref, co_ref, wx_ref, tgt_ref, sem
):
    nleaf = co_m.shape[0]
    nz, count, nvec = out_ref.shape[:3]
    nall = nz * nvec
    own_at = list_ref.shape[1] - 1 - nz
    copies = []
    for n, (src, dst) in enumerate(
        ((co_l, co_ref), (co_m, co_ref), (co_r, co_ref), (wx_l, wx_ref), (wx_m, wx_ref), (wx_r, wx_ref))
    ):
        copies.append(
            pltpu.make_async_copy(src, dst.at[pl.ds((n % 3) * nleaf, nleaf)], sem.at[n])
        )
        copies[-1].start()
    co_ref[3 * nleaf] = jnp.zeros(co_ref.shape[1:], F32)
    wx_ref[3 * nleaf] = jnp.zeros(wx_ref.shape[1:], F32)
    for c in copies:
        c.wait()

    def target(t, carry):
        own = jnp.transpose(co_ref[list_ref[t, own_at]])
        for c in range(3):
            tgt_ref[c] = jnp.broadcast_to(own[:, c : c + 1], (128, 128))

        def step(k, acc):
            for g in range(NEAR_STEP):
                his, los, ws = [], [], []
                for s in range(2):
                    m = list_ref[t, 2 * (k * NEAR_STEP + g) + s]
                    co = co_ref[m]
                    d0 = tgt_ref[0] - co[0:1]
                    d1 = tgt_ref[1] - co[1:2]
                    d2 = tgt_ref[2] - co[2:3]
                    kern = lax.rsqrt(d0 * d0 + d1 * d1 + (d2 * d2 + SOFT_SQ))
                    hi, lo = split(kern)
                    his.append(hi)
                    los.append(lo)
                    whi, wlo = split(wx_ref[m])
                    ws.append(jnp.concatenate([whi, wlo], axis=0))
                rhs = jnp.concatenate(
                    [jnp.concatenate(his, axis=1), jnp.concatenate(los, axis=1)], axis=0
                )
                acc = acc + dot(jnp.concatenate(ws, axis=1), rhs, NT)
            return acc

        acc = lax.fori_loop(0, list_ref[t, own_at - 1], step, jnp.zeros((2 * nall, 256), F32))
        x = acc[:nall, :128] + acc[nall:, :128] + acc[:nall, 128:]
        for k in range(nz):
            out_ref[list_ref[t, own_at + 1 + k], t] = x[k * nvec : (k + 1) * nvec]
        return carry

    lax.fori_loop(0, count, target, 0)


def shift_both(x, axis):
    ends = lax.axis_size(axis) - 1
    from_left = lax.ppermute(x, axis, [(i, i + 1) for i in range(ends)])
    from_right = lax.ppermute(x, axis, [(i + 1, i) for i in range(ends)])
    return from_left, from_right


def body(vectors, coords, weights, basis, transfer, coupling, far_leaf, far_parent, near_leaf):
    nleaf, rank, width = basis.shape
    nvec = vectors.shape[0]
    npar = nleaf // 8
    noff = coupling.shape[0]
    nz = lax.axis_size("vec")
    vec = lax.axis_index("vec")
    first = (lax.axis_index("leaf") - 1) * nleaf
    first_par = (lax.axis_index("leaf") - 1) * npar
    count = nleaf // nz
    nall = nvec * nz
    slots = near_leaf.shape[1]

    leaf_x = vectors.reshape(nvec, nleaf, width).transpose(1, 0, 2)
    leaf_w = (weights * (1.0 / (4.0 * math.pi))).reshape(nleaf, 1, width)
    piece = leaf_x * leaf_w
    pieces = [piece] + [
        lax.ppermute(piece, "vec", [(i, (i + k) % nz) for i in range(nz)]) for k in range(1, nz)
    ]
    wx = jnp.concatenate(pieces, axis=1)
    co = jnp.pad(coords.reshape(3, nleaf, width).transpose(1, 0, 2), ((0, 0), (0, 5), (0, 0)))
    co_l, co_r = shift_both(co, "leaf")

    params = pltpu.CompilerParams(vmem_limit_bytes=VMEM_BYTES)
    coeff = pl.pallas_call(
        up_kernel,
        out_shape=jax.ShapeDtypeStruct((nleaf, nvec, rank), F32),
        compiler_params=params,
        name="up",
        cost_estimate=pl.CostEstimate(flops=10**8, bytes_accessed=4 * 10**6, transcendentals=0),
    )(leaf_x, basis)
    coeff = coeff.reshape(nleaf, nvec * rank)
    c_l, c_r = shift_both(coeff, "leaf")
    wx_l, wx_r = shift_both(wx, "leaf")

    rows = -(-(nleaf + npar) // 16) * 16
    padded = -(-noff // FAR_STEP) * FAR_STEP
    depth = 256
    cols = nvec * rank
    far_out = pl.pallas_call(
        far_kernel,
        out_shape=jax.ShapeDtypeStruct((nvec, nleaf * width), F32),
        scratch_shapes=[
            pltpu.VMEM((cols // 128, depth, 128), F32),
            pltpu.VMEM((depth, 2 * cols), BF16),
            pltpu.VMEM((cols // 128, nleaf, 128), F32),
            pltpu.VMEM((-(-noff // 128), rows, 128), jnp.int32),
            pltpu.VMEM((padded * rank, 128), F32),
        ],
        compiler_params=params,
        name="far",
        cost_estimate=pl.CostEstimate(flops=10**10, bytes_accessed=10**8, transcendentals=0),
    )(c_l, coeff, c_r, transfer, coupling.transpose(1, 2, 0), far_leaf, far_parent, basis)

    mine = lax.dynamic_slice_in_dim(near_leaf, vec * count, count, axis=0)
    live = mine >= 0
    at = jnp.arange(slots)
    place = jnp.sum(live[:, None, :] & (at[None, None, :] < at[None, :, None]), axis=2)
    empty = 3 * nleaf
    group = 2 * NEAR_STEP
    j = jnp.arange(-(-slots // group) * group)
    lists = empty + jnp.sum(
        jnp.where(
            live[:, None, :] & (place[:, None, :] == j[None, :, None]),
            (mine - first - empty)[:, None, :],
            0,
        ),
        axis=2,
    )
    steps = (jnp.sum(live, axis=1) + group - 1) // group
    own = nleaf + vec * count + jnp.arange(count)
    lists = jnp.concatenate(
        [lists, steps[:, None], own[:, None], jnp.broadcast_to((vec - jnp.arange(nz)) % nz, (count, nz))],
        axis=1,
    ).astype(jnp.int32)
    anywhere = pl.BlockSpec(memory_space=pl.ANY)
    near = pl.pallas_call(
        near_kernel,
        out_shape=jax.ShapeDtypeStruct((nz, count, nvec, width), F32),
        in_specs=[pl.BlockSpec(memory_space=pltpu.SMEM)] + [anywhere] * 6,
        scratch_shapes=[
            pltpu.VMEM((3 * nleaf + 1, 8, width), F32),
            pltpu.VMEM((3 * nleaf + 1, nall, width), F32),
            pltpu.VMEM((3, width, width), F32),
            pltpu.SemaphoreType.DMA((6,)),
        ],
        compiler_params=params,
        name="near",
        cost_estimate=pl.CostEstimate(flops=10**10, bytes_accessed=10**8, transcendentals=0),
    )(lists, co_l, co, co_r, wx_l, wx, wx_r)
    near = lax.all_to_all(near, "vec", split_axis=0, concat_axis=0, tiled=True)
    near = near.reshape(nleaf, nvec, width)
    return far_out + near.transpose(1, 0, 2).reshape(nvec, nleaf * width)


def solution(mesh):
    in_specs = (
        P("vec", ("groups", "leaf")),
        P(None, ("groups", "leaf")),
        P(("groups", "leaf")),
        P(("groups", "leaf"), None, None),
        P(),
        P(),
        P(("groups", "leaf"), None),
        P(("groups", "leaf"), None),
        P(("groups", "leaf"), None),
    )
    out_specs = P("vec", ("groups", "leaf"))
    return jax.shard_map(body, mesh=mesh, in_specs=in_specs, out_specs=out_specs, check_vma=False)
```
